32 devices in a mesh: groups: 2 (over x), expert: 16 (over z, y, core).
Axes of the slice: x: 2, y: 2, z: 4, core: 2. Of those that a mesh axis runs over, the one named last changes fastest.
Arguments:
- tokens: bfloat16 [8192, 1024], P(('groups', 'expert')), parts along dimension 0, may hold values from -6 to 6
- expert_ids: int32 [8192, 2], P(('groups', 'expert')), parts along dimension 0, may hold values from 0 to 15, as said below
- gate_weights: float32 [8192, 2], P(('groups', 'expert')), parts along dimension 0, may hold values from 0.2 to 1
- out_grad: bfloat16 [8192, 1024], P(('groups', 'expert')), parts along dimension 0, may hold values from -6 to 6
- w_in: bfloat16 [16, 1024, 2048], P('expert'), may hold values from -0.1875 to 0.1875
- w_out: bfloat16 [16, 2048, 1024], P('expert'), may hold values from -0.125 to 0.125
Outputs:
- moe_out: bfloat16 [8192, 1024], P(('groups', 'expert')), parts along dimension 0
- token_grad: bfloat16 [8192, 1024], P(('groups', 'expert')), parts along dimension 0
- w_in_grad: bfloat16 [32, 1024, 2048], P(('groups', 'expert')), parts along dimension 0
- w_out_grad: bfloat16 [32, 2048, 1024], P(('groups', 'expert')), parts along dimension 0
The draws below stay inside these ranges and needn't reach their ends.
There are 2 independent parts, one for each index of `groups`. The reference program is written for one: setup_inputs(seed, part) draws one part's arguments, and reference() takes and returns one part's arrays. A program takes and returns all parts, laid end to end along the dimension named above; an argument that names none is the same for every part. Nothing has to cross between parts.
Inputs may be any that keep to these rules, and one draw needn't show every extreme that they name: `expert_ids`: each token names two different experts. Among the 256 tokens of one device, one expert, the same for all devices of a part, is named by exactly 96 tokens, and no expert by more than 96.
All inputs are finite; a program needn't handle non-finite values.
Results may differ from the reference program's by a relative error of at most 0.0065.
Values may be sent and summed in bfloat16 or wider, within the bound.
No kernel may reach another device: no remote copies, remote signals or barrier semaphores. Data moves between devices by JAX's collectives and lax.ppermute only.
A program may use at most 128 MiB of HBM per device.

```python
import jax
import jax.numpy as jnp
from jax import lax

D = 1024
FF = 2048
TOK_DEV = 256
TOKENS = 4096
EXPERTS = 16
CAP = 96
N_EXPERT = 16


def draw_expert_ids(key, part):
    key = jax.random.fold_in(key, 11)
    rest_count = EXPERTS - 2
    hot_expert = jax.random.randint(jax.random.fold_in(key, 1), (), 0, EXPERTS)
    all_experts = jnp.arange(EXPERTS, dtype=jnp.int32)
    positions = jnp.arange(TOK_DEV, dtype=jnp.int32)

    def one_block(block_index):
        block_key = jax.random.fold_in(key, block_index + 100)
        keys_list = jax.random.split(block_key, 6)
        warm_expert = (hot_expert + 1 + jax.random.randint(keys_list[0], (), 0, EXPERTS - 1)) % EXPERTS
        marks = ((all_experts == hot_expert) | (all_experts == warm_expert)).astype(jnp.int32)
        rest_sorted = jnp.sort(all_experts + EXPERTS * marks)[:rest_count]
        rest_experts = rest_sorted[jax.random.permutation(keys_list[1], rest_count)]
        warm_count = jax.random.randint(keys_list[2], (), 0, CAP + 1)
        shift_extra = jax.random.randint(keys_list[3], (), 0, rest_count - 1)
        first_pick = jnp.where(positions < CAP, hot_expert, jnp.where(positions < CAP + warm_count, warm_expert, rest_experts[positions % rest_count]))
        second_pick = jnp.where(positions < CAP + warm_count, rest_experts[positions % rest_count], rest_experts[(positions + 1 + shift_extra) % rest_count])
        pairs = jnp.stack([first_pick, second_pick], axis=1)
        pairs = pairs[jax.random.permutation(keys_list[4], TOK_DEV)]
        slot_flip = jax.random.randint(keys_list[5], (TOK_DEV, 1), 0, 2)
        return jnp.where(slot_flip == 1, pairs[:, ::-1], pairs)
    blocks = jax.vmap(one_block)(jnp.arange(N_EXPERT, dtype=jnp.int32))
    return blocks.reshape(TOKENS, 2).astype(jnp.int32)


def block_scale(own_key, dims, pieces, least, high):
    factor_of = 1.0
    for axis_at, parts in pieces:
        heights = jax.random.uniform(jax.random.fold_in(jax.random.fold_in(own_key, 6), axis_at), (parts,), jnp.float32, least / len(pieces), high / len(pieces))
        factor_of = factor_of * jnp.repeat(jnp.exp(heights), dims[axis_at] // parts).reshape((-1,) + (1,) * (len(dims) - 1 - axis_at))
    return factor_of


def centred(own_key, shape, spread, reach, shards=(), held_as=jnp.bfloat16):
    result = jax.random.normal(own_key, shape, jnp.float32) * spread
    if len(shards) > 0:
        result = block_scale(own_key, shape, shards, -0.22, 0.18) * result
    return jnp.clip(result, min=-reach, max=reach).astype(held_as)


def setup_inputs(seed: int = 0, part: int = 0) -> dict:
    seeds = jax.random.split(jax.random.key(seed), 7)
    own_keys = jax.random.split(jax.random.fold_in(seeds[6], part), 7)
    tokens = centred(own_keys[0], (TOKENS, D), 1.0, 6.0, ((0, 16),))
    expert_ids = draw_expert_ids(jax.random.fold_in(jax.random.fold_in(seeds[6], part), 71), part)
    gate_weights = jnp.clip(0.2 + 0.8 * jax.random.uniform(own_keys[2], (TOKENS, 2), jnp.float32) ** block_scale(own_keys[2], (TOKENS, 2), ((0, 16),), -0.2, 0.2), 0.2, 1.0)
    out_grad = centred(own_keys[3], (TOKENS, D), 1.0, 6.0, ((0, 16),))
    w_in = centred(seeds[4], (EXPERTS, D, FF), D ** -0.5, 0.1875, ((0, 16),))
    w_out = centred(seeds[5], (EXPERTS, FF, D), FF ** -0.5, 0.125, ((0, 16),))
    return dict(tokens=tokens, expert_ids=expert_ids, gate_weights=gate_weights, out_grad=out_grad, w_in=w_in, w_out=w_out)


INV_ROOT_TWO = 0.7071067811865476
INV_ROOT_TAU = 0.3989422804014327


def gelu_parts(pre_act):
    normal_cdf = 0.5 * (1.0 + lax.erf(pre_act * INV_ROOT_TWO))
    normal_pdf = jnp.exp(-0.5 * pre_act * pre_act) * INV_ROOT_TAU
    return pre_act * normal_cdf, normal_cdf + pre_act * normal_pdf


def expert_pass(x_block, grad_block, weight_in, weight_out):
    pre_act = jnp.dot(x_block, weight_in, preferred_element_type=jnp.float32)
    activation, gelu_slope = gelu_parts(pre_act)
    activation = activation.astype(jnp.bfloat16)
    expert_out = jnp.dot(activation, weight_out, preferred_element_type=jnp.float32).astype(jnp.bfloat16)
    act_grad = lax.dot_general(grad_block, weight_out, (((1,), (1,)), ((), ())), preferred_element_type=jnp.float32)
    pre_grad = (act_grad * gelu_slope).astype(jnp.bfloat16)
    row_grad = lax.dot_general(pre_grad, weight_in, (((1,), (1,)), ((), ())), preferred_element_type=jnp.float32).astype(jnp.bfloat16)
    grad_out = lax.dot_general(activation, grad_block, (((0,), (0,)), ((), ())), preferred_element_type=jnp.float32)
    grad_in = lax.dot_general(x_block, pre_grad, (((0,), (0,)), ((), ())), preferred_element_type=jnp.float32)
    return expert_out, row_grad, grad_in, grad_out


def slot_ranks(expert_flat, expert_count):
    one_hot = (expert_flat[:, None] == jnp.arange(expert_count, dtype=jnp.int32)[None, :]).astype(jnp.int32)
    before = (jnp.cumsum(one_hot, axis=0) - one_hot).astype(jnp.int32)
    return jnp.sum(before * one_hot, axis=1).astype(jnp.int32)


def reference(tokens, expert_ids, gate_weights, out_grad, w_in, w_out):
    assign_count = 2 * TOKENS
    per_expert = N_EXPERT * CAP
    flat_ids = expert_ids.reshape(-1).astype(jnp.int32)
    slot_rank = slot_ranks(flat_ids, EXPERTS)
    slot_index = (flat_ids * per_expert + slot_rank).astype(jnp.int32)
    slot_source = jnp.full((EXPERTS * per_expert,), assign_count, jnp.int32).at[slot_index].set(jnp.arange(assign_count, dtype=jnp.int32))
    zero_row = jnp.zeros((1, D), jnp.bfloat16)
    x_rows = jnp.concatenate([jnp.repeat(tokens, 2, axis=0), zero_row], axis=0)
    scaled = (gate_weights.reshape(-1, 1) * jnp.repeat(out_grad, 2, axis=0).astype(jnp.float32)).astype(jnp.bfloat16)
    grad_rows = jnp.concatenate([scaled, zero_row], axis=0)

    def one_expert(expert):
        picked = lax.dynamic_slice_in_dim(slot_source, expert * per_expert, per_expert)
        return expert_pass(x_rows[picked], grad_rows[picked], w_in[expert], w_out[expert])

    expert_out, row_grad, grad_in, grad_out = lax.map(one_expert, jnp.arange(EXPERTS, dtype=jnp.int32))
    out_rows = expert_out.reshape(-1, D)[slot_index].reshape(TOKENS, 2, D).astype(jnp.float32)
    moe_out = jnp.sum(gate_weights[:, :, None] * out_rows, axis=1).astype(jnp.bfloat16)
    back_rows = row_grad.reshape(-1, D)[slot_index].reshape(TOKENS, 2, D).astype(jnp.float32)
    token_grad = jnp.sum(back_rows, axis=1).astype(jnp.bfloat16)
    return moe_out, token_grad, grad_in.astype(jnp.bfloat16), grad_out.astype(jnp.bfloat16)
```

```python
import functools

import jax
import jax.numpy as jnp
from jax import lax
from jax.experimental import pallas as pl
from jax.experimental.pallas import tpu as pltpu
from jax.sharding import PartitionSpec as P

AXIS = "expert"
PLANE = 4
INV_ROOT_TWO = 0.7071067811865476
INV_ROOT_TAU = 0.3989422804014327
BF16 = jnp.bfloat16
F32 = jnp.float32
SMEM = pl.BlockSpec(memory_space=pltpu.SMEM)
VMEM = pl.BlockSpec(memory_space=pltpu.VMEM)


def params(mib):
    return pltpu.CompilerParams(vmem_limit_bytes=mib * 1024 * 1024)


def dot(a, b, dims):
    return lax.dot_general(a, b, (dims, ((), ())), preferred_element_type=F32)


def slot_source(z, slot, length):
    near = min(z, length - 1 - z)
    far_up = z < length - 1 - z
    if slot <= 2 * near:
        return (slot + 1) // 2, far_up == (slot % 2 == 1)
    return slot - near, far_up


def slot_of(z, t, up, length):
    for slot in range(1, length):
        if slot_source(z, slot, length) == (t, up):
            return slot
    return None


def choose(z, values, pick):
    used = sorted({p for p in pick if p is not None})
    result = values[used[0]]
    for p in used[1:]:
        here = functools.reduce(jnp.logical_or, [z == k for k, q in enumerate(pick) if q == p])
        result = jnp.where(here, values[p], result)
    return result


def route_kernel(slots, cap, where_ref, meta_ref, pick_ref, put_ref, row_gate_ref, token_gate_ref):
    z, lo = where_ref[0], where_ref[1]
    length, _, tokens = meta_ref.shape
    upper = (
        lax.broadcasted_iota(jnp.int32, (tokens, tokens), 0)
        < lax.broadcasted_iota(jnp.int32, (tokens, tokens), 1)
    ).astype(BF16)
    eye = lax.broadcasted_iota(jnp.int32, (tokens, tokens), 0) == lax.broadcasted_iota(
        jnp.int32, (tokens, tokens), 1
    )
    down = lax.broadcasted_iota(jnp.int32, (cap, tokens), 0).astype(F32)
    along = lax.broadcasted_iota(jnp.int32, (tokens, cap), 1).astype(F32)
    lane = lax.broadcasted_iota(jnp.int32, (tokens, 128), 1)
    for at, slot in enumerate(slots):
        block = meta_ref[where_ref[2 + slot]]
        first, second = block[0:1], block[1:2]
        gate_one, gate_two = block[2:3], block[3:4]
        marks, gates = [], []
        for peer in range(PLANE):
            expert = (z * PLANE + (lo ^ peer)).astype(F32)
            is_one = (first == expert).astype(F32)
            is_two = (second == expert).astype(F32)
            marks.append(is_one + is_two)
            gates.append(is_one * gate_one + is_two * gate_two)
        marks = jnp.concatenate(marks + marks, axis=0)
        rank = dot(marks.astype(BF16), upper, ((1,), (0,)))
        rank = jnp.where(marks > 0.0, rank, -1.0)
        token_gate = jnp.zeros((tokens, 128), F32)
        for peer in range(PLANE):
            row = rank[peer : peer + 1]
            hit = down == row
            pick_ref[at, peer] = hit.astype(F32).astype(BF16)
            gate = jnp.sum(jnp.where(hit, gates[peer], 0.0), axis=1, keepdims=True)
            row_gate_ref[at, peer] = jnp.broadcast_to(gate, (cap, 128))
            column = jnp.sum(jnp.where(eye, row, 0.0), axis=1, keepdims=True)
            put_ref[at, peer] = (along == column).astype(F32).astype(BF16)
            gate = jnp.sum(jnp.where(eye, gates[peer], 0.0), axis=1, keepdims=True)
            token_gate = jnp.where(lane == peer, gate, token_gate)
        token_gate_ref[at] = token_gate


def route(where, meta, slots, cap):
    _, _, tokens = meta.shape
    count = len(slots)
    return pl.pallas_call(
        functools.partial(route_kernel, slots, cap),
        out_shape=(
            jax.ShapeDtypeStruct((count, PLANE, cap, tokens), BF16),
            jax.ShapeDtypeStruct((count, PLANE, tokens, cap), BF16),
            jax.ShapeDtypeStruct((count, PLANE, cap, 128), F32),
            jax.ShapeDtypeStruct((count, tokens, 128), F32),
        ),
        in_specs=[SMEM, VMEM],
        out_specs=(VMEM,) * 4,
        compiler_params=params(32),
        cost_estimate=pl.CostEstimate(flops=10**7, bytes_accessed=10**6, transcendentals=0),
        name="route",
    )(where, meta)


def select_kernel(pick, scaled, where_ref, *refs):
    blocks = refs[: len(refs) - 2 - PLANE]
    pick_ref, row_gate_ref = refs[len(blocks) : len(blocks) + 2]
    outs = refs[len(blocks) + 2 :]
    block = choose(where_ref[0], [r[...] for r in blocks], pick)
    for peer in range(PLANE):
        rows = dot(pick_ref[0, peer], block, ((1,), (0,)))
        if scaled:
            rows = rows * row_gate_ref[0, peer][:, :1]
        outs[peer][...] = rows.astype(BF16)


def select(where, blocks, pick, routes, at, scaled):
    picks, _, row_gates, _ = routes
    _, _, cap, tokens = picks.shape
    width = blocks[0].shape[1]
    return pl.pallas_call(
        functools.partial(select_kernel, pick, scaled),
        grid=(1,),
        out_shape=(jax.ShapeDtypeStruct((cap, width), BF16),) * PLANE,
        in_specs=[SMEM]
        + [pl.BlockSpec(b.shape, lambda i: (0, 0)) for b in blocks]
        + [
            pl.BlockSpec((1, PLANE, cap, tokens), lambda i: (at, 0, 0, 0)),
            pl.BlockSpec((1, PLANE, cap, 128), lambda i: (at, 0, 0, 0)),
        ],
        out_specs=(pl.BlockSpec((cap, width), lambda i: (0, 0)),) * PLANE,
        compiler_params=params(40),
        cost_estimate=pl.CostEstimate(
            flops=2 * PLANE * cap * tokens * width,
            bytes_accessed=4 * 10**6,
            transcendentals=0,
        ),
        name="select_rows",
    )(where, *blocks, picks, row_gates)


def combine_kernel(pick, slots, gated, extras, where_ref, *refs):
    rows = [refs[PLANE * k : PLANE * (k + 1)] for k in range(len(slots))]
    rest = refs[PLANE * len(slots) :]
    puts, rest = rest[: len(slots)], rest[len(slots) :]
    gates, rest = rest[: len(slots)], rest[len(slots) :]
    more, out_ref = rest[:extras], rest[extras]
    z = where_ref[0]
    total = None
    for ref in more:
        value = ref[...].astype(F32)
        total = value if total is None else total + value
    gate = choose(z, [g[0] for g in gates], pick)
    for peer in range(PLANE):
        put = choose(z, [p[0, peer] for p in puts], pick)
        row = choose(z, [r[peer][...] for r in rows], pick)
        part = dot(put, row, ((1,), (0,)))
        if gated:
            part = part * gate[:, peer : peer + 1]
        total = part if total is None else total + part
    out_ref[...] = total.astype(BF16)


def combine(where, rows, routes, pick, gated, extras):
    slots = sorted({p for p in pick if p is not None})
    pick = [None if p is None else slots.index(p) for p in pick]
    cap, width = rows[slots[0]][0].shape
    tokens = routes[slots[0]][0][1].shape[2]
    operands, specs = [], []
    for s in slots:
        operands += list(rows[s])
        specs += [pl.BlockSpec((cap, width), lambda i: (0, 0))] * PLANE
    for s in slots:
        found, at = routes[s]
        operands.append(found[1])
        specs.append(
            pl.BlockSpec((1, PLANE, tokens, cap), functools.partial(lambda a, i: (a, 0, 0, 0), at))
        )
    for s in slots:
        found, at = routes[s]
        operands.append(found[3])
        specs.append(pl.BlockSpec((1, tokens, 128), functools.partial(lambda a, i: (a, 0, 0), at)))
    operands += list(extras)
    specs += [pl.BlockSpec((tokens, width), lambda i: (0, 0))] * len(extras)
    return pl.pallas_call(
        functools.partial(combine_kernel, pick, slots, gated, len(extras)),
        grid=(1,),
        out_shape=jax.ShapeDtypeStruct((tokens, width), BF16),
        in_specs=[SMEM] + specs,
        out_specs=pl.BlockSpec((tokens, width), lambda i: (0, 0)),
        compiler_params=params(40),
        cost_estimate=pl.CostEstimate(
            flops=2 * PLANE * cap * tokens * width,
            bytes_accessed=4 * 10**6,
            transcendentals=0,
        ),
        name="combine_rows",
    )(where, *operands)


def gelu_parts(pre_act):
    normal_cdf = 0.5 * (1.0 + lax.erf(pre_act * INV_ROOT_TWO))
    normal_pdf = jnp.exp(-0.5 * pre_act * pre_act) * INV_ROOT_TAU
    return (pre_act * normal_cdf, normal_cdf + pre_act * normal_pdf)


def gather_pieces(cap, pieces, whole_ref):
    for k, ref in enumerate(pieces):
        whole_ref[k * cap : (k + 1) * cap, :] = ref[...]


def forward_kernel(cap, steps, *refs):
    pieces, (win_ref, wout_ref) = refs[:PLANE], refs[PLANE : PLANE + 2]
    outs = refs[PLANE + 2 : 2 * PLANE + 2]
    x_ref, act_ref, slope_ref, total = refs[2 * PLANE + 2 :]
    step = pl.program_id(0)

    @pl.when(step == 0)
    def _():
        gather_pieces(cap, pieces, x_ref)

    pre_act = dot(x_ref[...], win_ref[0], ((1,), (0,)))
    act, slope = gelu_parts(pre_act)
    act = act.astype(BF16)
    act_ref[...] = act
    slope_ref[...] = slope
    part = dot(act, wout_ref[0], ((1,), (0,)))

    @pl.when(step == 0)
    def _():
        total[...] = part

    @pl.when(step > 0)
    def _():
        total[...] += part

    @pl.when(step == steps - 1)
    def _():
        for k, ref in enumerate(outs):
            ref[...] = total[k * cap : (k + 1) * cap, :].astype(BF16)


def forward(pieces, w_in, w_out, tile=512):
    cap, width = pieces[0].shape
    hidden = w_in.shape[2]
    rows, steps = PLANE * cap, hidden // tile
    piece = pl.BlockSpec((cap, width), lambda f: (0, 0))
    result = pl.pallas_call(
        functools.partial(forward_kernel, cap, steps),
        grid=(steps,),
        out_shape=(jax.ShapeDtypeStruct((cap, width), BF16),) * PLANE
        + (
            jax.ShapeDtypeStruct((rows, width), BF16),
            jax.ShapeDtypeStruct((rows, hidden), BF16),
            jax.ShapeDtypeStruct((rows, hidden), F32),
        ),
        in_specs=[piece] * PLANE
        + [
            pl.BlockSpec((1, width, tile), lambda f: (0, 0, f)),
            pl.BlockSpec((1, tile, width), lambda f: (0, f, 0)),
        ],
        out_specs=(piece,) * PLANE
        + (
            pl.BlockSpec((rows, width), lambda f: (0, 0)),
            pl.BlockSpec((rows, tile), lambda f: (0, f)),
            pl.BlockSpec((rows, tile), lambda f: (0, f)),
        ),
        scratch_shapes=[pltpu.VMEM((rows, width), F32)],
        compiler_params=params(48),
        cost_estimate=pl.CostEstimate(
            flops=4 * rows * width * hidden,
            bytes_accessed=4 * width * hidden + 8 * rows * hidden,
            transcendentals=2 * rows * hidden,
        ),
        name="expert_forward",
    )(*pieces, w_in, w_out)
    return result[:PLANE], result[PLANE], result[PLANE + 1], result[PLANE + 2]


def backward_kernel(cap, steps, *refs):
    pieces, (win_ref, wout_ref, slope_ref) = refs[:PLANE], refs[PLANE : PLANE + 3]
    outs = refs[PLANE + 3 : 2 * PLANE + 3]
    grad_ref, pre_ref, total = refs[2 * PLANE + 3 :]
    step = pl.program_id(0)

    @pl.when(step == 0)
    def _():
        gather_pieces(cap, pieces, grad_ref)

    act_grad = dot(grad_ref[...], wout_ref[0], ((1,), (1,)))
    pre_grad = (act_grad * slope_ref[...]).astype(BF16)
    pre_ref[...] = pre_grad
    part = dot(pre_grad, win_ref[0], ((1,), (1,)))

    @pl.when(step == 0)
    def _():
        total[...] = part

    @pl.when(step > 0)
    def _():
        total[...] += part

    @pl.when(step == steps - 1)
    def _():
        for k, ref in enumerate(outs):
            ref[...] = total[k * cap : (k + 1) * cap, :].astype(BF16)


def backward(pieces, w_in, w_out, slope, tile=512):
    cap, width = pieces[0].shape
    hidden = w_in.shape[2]
    rows, steps = PLANE * cap, hidden // tile
    piece = pl.BlockSpec((cap, width), lambda f: (0, 0))
    result = pl.pallas_call(
        functools.partial(backward_kernel, cap, steps),
        grid=(steps,),
        out_shape=(jax.ShapeDtypeStruct((cap, width), BF16),) * PLANE
        + (
            jax.ShapeDtypeStruct((rows, width), BF16),
            jax.ShapeDtypeStruct((rows, hidden), BF16),
        ),
        in_specs=[piece] * PLANE
        + [
            pl.BlockSpec((1, width, tile), lambda f: (0, 0, f)),
            pl.BlockSpec((1, tile, width), lambda f: (0, f, 0)),
            pl.BlockSpec((rows, tile), lambda f: (0, f)),
        ],
        out_specs=(piece,) * PLANE
        + (
            pl.BlockSpec((rows, width), lambda f: (0, 0)),
            pl.BlockSpec((rows, tile), lambda f: (0, f)),
        ),
        scratch_shapes=[pltpu.VMEM((rows, width), F32)],
        compiler_params=params(48),
        cost_estimate=pl.CostEstimate(
            flops=4 * rows * width * hidden,
            bytes_accessed=4 * width * hidden + 6 * rows * hidden,
            transcendentals=0,
        ),
        name="expert_backward",
    )(*pieces, w_in, w_out, slope)
    return result[:PLANE], result[PLANE], result[PLANE + 1]


def weights_kernel(count, *refs):
    xs, pres = refs[:count], refs[count : 2 * count]
    acts, grads = refs[2 * count : 3 * count], refs[3 * count : 4 * count]
    gin_ref, gout_ref = refs[4 * count :]
    gin = gout = None
    for x, pre, act, grad in zip(xs, pres, acts, grads):
        part = dot(x[...], pre[...], ((0,), (0,)))
        gin = part if gin is None else gin + part
        part = dot(act[...], grad[...], ((0,), (0,)))
        gout = part if gout is None else gout + part
    gin_ref[0] = gin.astype(BF16)
    gout_ref[0] = gout.astype(BF16)


def weight_grads(xs, pres, acts, grads, tile=512):
    rows, width = xs[0].shape
    hidden = acts[0].shape[1]
    count = len(xs)
    whole = pl.BlockSpec((rows, width), lambda f: (0, 0))
    part = pl.BlockSpec((rows, tile), lambda f: (0, f))
    return pl.pallas_call(
        functools.partial(weights_kernel, count),
        grid=(hidden // tile,),
        out_shape=(
            jax.ShapeDtypeStruct((1, width, hidden), BF16),
            jax.ShapeDtypeStruct((1, hidden, width), BF16),
        ),
        in_specs=[whole] * count + [part] * (2 * count) + [whole] * count,
        out_specs=(
            pl.BlockSpec((1, width, tile), lambda f: (0, 0, f)),
            pl.BlockSpec((1, tile, width), lambda f: (0, f, 0)),
        ),
        compiler_params=params(56),
        cost_estimate=pl.CostEstimate(
            flops=4 * count * rows * width * hidden,
            bytes_accessed=4 * width * hidden + 4 * count * rows * (width + hidden),
            transcendentals=0,
        ),
        name="weight_grads",
    )(*xs, *pres, *acts, *grads)


def permute(value, pairs):
    return lax.ppermute(value, AXIS, pairs)


def shift_pairs(length, step, first, last):
    return [
        (z * PLANE + lo, (z + step) * PLANE + lo)
        for z in range(max(first, 0), min(last, length))
        if 0 <= z + step < length
        for lo in range(PLANE)
    ]


def to_peer(value, peer, count):
    return permute(value, [(i, i ^ peer) for i in range(count)])


def gather_line(block, length):
    got = {(0, True): block, (0, False): block}
    for t in range(1, length):
        got[t, False] = permute(got[t - 1, False], shift_pairs(length, 1, t - 1, length))
        got[t, True] = permute(got[t - 1, True], shift_pairs(length, -1, 0, length - t + 1))
    return got


def local(tokens, expert_ids, gate_weights, out_grad, w_in, w_out):
    count = lax.axis_size(AXIS)
    me = lax.axis_index(AXIS)
    length = count // PLANE
    tok_count, _ = tokens.shape
    cap = 6 * tok_count // count
    z, lo = me // PLANE, me % PLANE

    sources = []
    for slot in range(length):
        per_z = []
        for k in range(length):
            t, up = slot_source(k, slot, length) if slot else (0, True)
            per_z.append((-t if up else t) % length)
        sources.append(jnp.asarray(per_z, jnp.int32)[z])
    where = jnp.stack([z, lo] + sources).astype(jnp.int32)

    meta = jnp.concatenate([expert_ids.T.astype(F32), gate_weights.T], axis=0)
    ring = [meta]
    for t in range(1, length):
        pairs = [
            (k * PLANE + j, (k + t) % length * PLANE + j)
            for k in range(length)
            for j in range(PLANE)
        ]
        ring.append(permute(meta, pairs))
    own_routes = route(where, meta[None], (0,), cap)
    far_routes = route(where, jnp.stack(ring), tuple(range(1, length)), cap)
    routes = [(own_routes, 0)] + [(far_routes, s) for s in range(length - 1)]

    def dispatch(got, slot, scaled):
        found, at = routes[slot]
        if slot == 0:
            blocks, pick = [got[0, True]], [0] * length
        else:
            per_z = [slot_source(k, slot, length) for k in range(length)]
            keys = sorted(set(per_z))
            blocks, pick = [got[k] for k in keys], [keys.index(k) for k in per_z]
        parts = select(where, blocks, pick, found, at, scaled)
        return [parts[0]] + [to_peer(parts[p], p, count) for p in range(1, PLANE)]

    def give_back(parts):
        return [parts[0]] + [to_peer(parts[p], p, count) for p in range(1, PLANE)]

    def reduce_line(rows, gated):
        up_in = down_in = None
        for t in range(length - 1, 0, -1):
            sends = []
            for up, moving in ((True, up_in), (False, down_in)):
                pick = [slot_of(k, t, up, length) for k in range(length)]
                extras = [] if moving is None else [moving]
                sends.append(combine(where, rows, routes, pick, gated, extras))
            up_in = permute(sends[0], shift_pairs(length, 1, 0, length - t))
            down_in = permute(sends[1], shift_pairs(length, -1, t, length))
        return combine(where, rows, routes, [0] * length, gated, [up_in, down_in])

    slots = range(length)
    got_x = gather_line(tokens, length)
    x_parts = [dispatch(got_x, s, False) for s in slots]
    held, _ = lax.optimization_barrier((out_grad, got_x[max(length - 2, 1), True]))
    got_grad = gather_line(held, length)
    grad_parts = [dispatch(got_grad, s, True) for s in slots]

    outs, xs, acts, slopes = zip(*[forward(x_parts[s], w_in, w_out) for s in slots])
    out_rows = [None] * length
    for s in reversed(slots):
        out_rows[s] = give_back(outs[s])
    moe_out = reduce_line(out_rows, True)

    backs, grads, pres = zip(*[backward(grad_parts[s], w_in, w_out, slopes[s]) for s in slots])
    back_rows = [None] * length
    for s in reversed(slots):
        back_rows[s] = give_back(backs[s])
    token_grad = reduce_line(back_rows, False)

    w_in_grad, w_out_grad = weight_grads(xs, pres, acts, grads)
    return moe_out, token_grad, w_in_grad, w_out_grad


def solution(mesh):
    rows, wide = P(("groups", AXIS), None), P(("groups", AXIS), None, None)
    weights = P(AXIS, None, None)
    return jax.shard_map(
        local,
        mesh=mesh,
        in_specs=(rows, rows, rows, rows, weights, weights),
        out_specs=(rows, rows, wide, wide),
        check_vma=False,
    )
```

```python
import functools

import jax
import jax.numpy as jnp
from jax import lax
from jax.experimental import pallas as pl
from jax.experimental.pallas import tpu as pltpu
from jax.sharding import PartitionSpec as P

AXIS = "expert"
PLANE = 4
PAIR = 2
INV_ROOT_TWO = 0.7071067811865476
INV_ROOT_TAU = 0.3989422804014327
PEAK = 5.75e9
BF16 = jnp.bfloat16
F32 = jnp.float32
SMEM = pl.BlockSpec(memory_space=pltpu.SMEM)
VMEM = pl.BlockSpec(memory_space=pltpu.VMEM)


def params(mib):
    return pltpu.CompilerParams(vmem_limit_bytes=mib * 1024 * 1024)


def dot(a, b, dims):
    return lax.dot_general(a, b, (dims, ((), ())), preferred_element_type=F32)


META = 16


def call(
    kernel, order, operands, specs, out_shape, out_specs, name, mib=24, grid=(1,), scratch=(), cost=1.5
):
    result = pl.pallas_call(
        kernel,
        grid=grid,
        out_shape=out_shape,
        in_specs=specs,
        out_specs=out_specs,
        scratch_shapes=list(scratch),
        compiler_params=params(mib),
        cost_estimate=pl.CostEstimate(
            flops=int(cost * PEAK), bytes_accessed=1000, transcendentals=0
        ),
        name=name,
    )(*order.behind(operands))
    order.last = result[0] if isinstance(result, (tuple, list)) else result
    return result


class Order:
    def __init__(self):
        self.last = None

    def behind(self, operands):
        if self.last is None:
            return list(operands)
        return list(lax.optimization_barrier((tuple(operands), self.last))[0])


def whole(shape):
    zeros = (0,) * len(shape)
    return pl.BlockSpec(shape, lambda *i: zeros)


def stack_kernel(tokens_ref, ids_ref, gates_ref, out_ref):
    tokens, _ = tokens_ref.shape
    out_ref[:tokens, :] = tokens_ref[...]
    eye = lax.broadcasted_iota(jnp.int32, (tokens, tokens), 0) == lax.broadcasted_iota(
        jnp.int32, (tokens, tokens), 1
    )

    def as_row(column):
        return jnp.sum(jnp.where(eye, column, 0.0), axis=0, keepdims=True)

    ids, gates = ids_ref[...].astype(F32), gates_ref[...]
    rows = [as_row(ids[:, k : k + 1]) for k in range(2)]
    for k in range(2):
        rest = as_row(gates[:, k : k + 1])
        for _ in range(3):
            part = rest.astype(BF16).astype(F32)
            rows.append(part)
            rest = rest - part
    rows += rows
    out_ref[tokens:, :] = jnp.zeros((META, out_ref.shape[1]), BF16)
    out_ref[tokens:, :tokens] = jnp.concatenate(rows, axis=0).astype(BF16)


def stack_block(order, tokens, expert_ids, gate_weights):
    count, width = tokens.shape
    return call(
        stack_kernel,
        order,
        (tokens, expert_ids, gate_weights),
        [whole(tokens.shape), whole(expert_ids.shape), whole(gate_weights.shape)],
        jax.ShapeDtypeStruct((count + META, width), BF16),
        whole((count + META, width)),
        "stack_block",
    )


def route_rows(experts, meta, cap, at, pick_ref, put_ref, row_gate_ref, token_gate_ref):
    tokens = meta.shape[1]
    upper = (
        lax.broadcasted_iota(jnp.int32, (tokens, tokens), 0)
        < lax.broadcasted_iota(jnp.int32, (tokens, tokens), 1)
    ).astype(BF16)
    eye = lax.broadcasted_iota(jnp.int32, (tokens, tokens), 0) == lax.broadcasted_iota(
        jnp.int32, (tokens, tokens), 1
    )
    down = lax.broadcasted_iota(jnp.int32, (cap, tokens), 0).astype(F32)
    along = lax.broadcasted_iota(jnp.int32, (tokens, cap), 1).astype(F32)
    lane = lax.broadcasted_iota(jnp.int32, (tokens, 128), 1)
    first, second = meta[0:1], meta[1:2]
    gate_one = meta[2:3] + meta[3:4] + meta[4:5]
    gate_two = meta[5:6] + meta[6:7] + meta[7:8]
    marks, gates = [], []
    for expert in experts:
        is_one = (first == expert).astype(F32)
        is_two = (second == expert).astype(F32)
        marks.append(is_one + is_two)
        gates.append(is_one * gate_one + is_two * gate_two)
    marks = jnp.concatenate(marks * 4, axis=0)
    rank = dot(marks.astype(BF16), upper, ((1,), (0,)))
    rank = jnp.where(marks > 0.0, rank, -1.0)
    token_gate = jnp.zeros((tokens, 128), F32)
    picks = []
    for k in range(PAIR):
        row = rank[k : k + 1]
        hit = down == row
        picks.append(hit.astype(F32).astype(BF16))
        pick_ref[k, at] = picks[-1]
        gate = jnp.sum(jnp.where(hit, gates[k], 0.0), axis=1, keepdims=True)
        row_gate_ref[k, at] = jnp.broadcast_to(gate, (cap, 128))
        column = jnp.sum(jnp.where(eye, row, 0.0), axis=1, keepdims=True)
        put_ref[k, at] = (along == column).astype(F32).astype(BF16)
        gate = jnp.sum(jnp.where(eye, gates[k], 0.0), axis=1, keepdims=True)
        token_gate = jnp.where(lane == k, gate, token_gate)
    token_gate_ref[at] = token_gate
    return picks


def select_kernel(scaled, cap, me_ref, *refs):
    blocks, refs = refs[:PAIR], refs[PAIR:]
    if scaled:
        (pick_ref, row_gate_ref), refs = refs[:2], refs[2:]
    outs, routes = refs[:PAIR], refs[PAIR:]
    me = me_ref[0]
    experts = [me.astype(F32), (me ^ 2).astype(F32)]
    for at, ref in enumerate(blocks):
        if scaled:
            block = ref[...]
            picks = [pick_ref[k, at] for k in range(PAIR)]
        else:
            tokens = ref.shape[0] - META
            block = ref[:tokens, :]
            meta = ref[tokens:, :tokens].astype(F32)
            picks = route_rows(experts, meta, cap, at, *routes)
        for k in range(PAIR):
            rows = dot(picks[k], block, ((1,), (0,)))
            if scaled:
                rows = rows * row_gate_ref[k, at][:, :1]
            outs[k][at * cap : (at + 1) * cap, :] = rows.astype(BF16)


def select(order, me, blocks, cap, routes=None):
    width = blocks[0].shape[1]
    tokens = blocks[0].shape[0] - (META if routes is None else 0)
    shapes = [jax.ShapeDtypeStruct((PAIR * cap, width), BF16)] * PAIR
    operands = [me, *blocks]
    specs = [SMEM] + [whole(b.shape) for b in blocks]
    if routes is None:
        shapes += [
            jax.ShapeDtypeStruct((PAIR, PAIR, cap, tokens), BF16),
            jax.ShapeDtypeStruct((PAIR, PAIR, tokens, cap), BF16),
            jax.ShapeDtypeStruct((PAIR, PAIR, cap, 128), F32),
            jax.ShapeDtypeStruct((PAIR, tokens, 128), F32),
        ]
    else:
        operands += [routes[0], routes[2]]
        specs += [whole(routes[0].shape), whole(routes[2].shape)]
    result = call(
        functools.partial(select_kernel, routes is not None, cap),
        order,
        operands,
        specs,
        tuple(shapes),
        tuple(whole(s.shape) for s in shapes),
        "select_rows",
    )
    return result[:PAIR], result[PAIR:]


def combine_kernel(at, gated, *refs):
    rows, (put_ref, gate_ref), more, out_ref = refs[:PAIR], refs[PAIR : PAIR + 2], refs[PAIR + 2 : -1], refs[-1]
    cap = rows[0].shape[0] // PAIR
    total = None
    for k in range(PAIR):
        part = dot(put_ref[k, at], rows[k][at * cap : (at + 1) * cap, :], ((1,), (0,)))
        if gated:
            part = part * gate_ref[at][:, k : k + 1]
        total = part if total is None else total + part
    for ref in more:
        total = total + ref[...].astype(F32)
    out_ref[...] = total.astype(BF16)


def combine(order, rows, routes, at, gated, extras=()):
    operands = [*rows, routes[1], routes[3], *extras]
    shape = (routes[3].shape[1], rows[0].shape[1])
    return call(
        functools.partial(combine_kernel, at, gated),
        order,
        operands,
        [whole(o.shape) for o in operands],
        jax.ShapeDtypeStruct(shape, BF16),
        whole(shape),
        "combine_rows",
    )


def gelu_parts(pre_act):
    normal_cdf = 0.5 * (1.0 + lax.erf(pre_act * INV_ROOT_TWO))
    normal_pdf = jnp.exp(-0.5 * pre_act * pre_act) * INV_ROOT_TAU
    return (pre_act * normal_cdf, normal_cdf + pre_act * normal_pdf)


def expert_kernel(first, steps, mine_ref, side_ref, win_ref, wout_ref, *refs):
    step = pl.program_id(0)
    if first:
        my_out, side_out, rows_ref, act_ref, slope_ref, total = refs
    else:
        slope_ref, my_out, side_out, rows_ref, pre_ref, total = refs
    size = mine_ref.shape[0]

    @pl.when(step == 0)
    def _():
        rows_ref[:size, :] = mine_ref[...]
        rows_ref[size:, :] = side_ref[...]
        total[...] = jnp.zeros_like(total)

    if first:
        act, slope = gelu_parts(dot(rows_ref[...], win_ref[0], ((1,), (0,))))
        act = act.astype(BF16)
        act_ref[...] = act
        slope_ref[...] = slope
        total[...] += dot(act, wout_ref[0], ((1,), (0,)))
    else:
        act_grad = dot(rows_ref[...], wout_ref[0], ((1,), (1,)))
        pre_grad = (act_grad * slope_ref[...]).astype(BF16)
        pre_ref[...] = pre_grad
        total[...] += dot(pre_grad, win_ref[0], ((1,), (1,)))

    @pl.when(step == steps - 1)
    def _():
        my_out[...] = total[:size, :].astype(BF16)
        side_out[...] = total[size:, :].astype(BF16)


def expert_pass(order, mine, side, w_in, w_out, slope=None, tile=512):
    first = slope is None
    width, hidden = w_in.shape[1:]
    size = mine.shape[0]
    steps = hidden // tile
    part = pl.BlockSpec((2 * size, tile), lambda f: (0, f))
    shapes = [jax.ShapeDtypeStruct((size, width), BF16)] * 2
    shapes += [jax.ShapeDtypeStruct((2 * size, width), BF16)]
    shapes += [jax.ShapeDtypeStruct((2 * size, hidden), BF16)]
    shapes += [jax.ShapeDtypeStruct((2 * size, hidden), F32)] if first else []
    result = call(
        functools.partial(expert_kernel, first, steps),
        order,
        [mine, side, w_in, w_out] + ([] if first else [slope]),
        [whole(mine.shape), whole(side.shape)]
        + [
            pl.BlockSpec((1, width, tile), lambda f: (0, 0, f)),
            pl.BlockSpec((1, tile, width), lambda f: (0, f, 0)),
        ]
        + ([] if first else [part]),
        tuple(shapes),
        tuple(whole(k.shape) for k in shapes[:3]) + (part,) * (len(shapes) - 3),
        "expert_forward" if first else "expert_backward",
        mib=32,
        grid=(steps,),
        scratch=[pltpu.VMEM((2 * size, width), F32)],
        cost=5.0,
    )
    return result[:2], result[2:]


def weight_kernel(count, *refs):
    total = None
    for a, b in zip(refs[:count], refs[count : 2 * count]):
        part = dot(a[...], b[...], ((0,), (0,)))
        total = part if total is None else total + part
    refs[-1][0] = total.astype(BF16)


def weight_grad(order, lefts, rights, tile, by_left, name):
    m, n = lefts[0].shape[1], rights[0].shape[1]

    def spec(array, tiled):
        rows, columns = array.shape
        if tiled:
            return pl.BlockSpec((rows, tile), lambda f: (0, f))
        return pl.BlockSpec((rows, columns), lambda f: (0, 0))

    return call(
        functools.partial(weight_kernel, len(lefts)),
        order,
        [*lefts, *rights],
        [spec(a, by_left) for a in lefts] + [spec(b, not by_left) for b in rights],
        jax.ShapeDtypeStruct((1, m, n), BF16),
        pl.BlockSpec((1, tile, n), lambda f: (0, f, 0))
        if by_left
        else pl.BlockSpec((1, m, tile), lambda f: (0, 0, f)),
        name,
        mib=44,
        cost=10.0,
        grid=((m if by_left else n) // tile,),
    )


def permute(value, pairs):
    return lax.ppermute(value, AXIS, pairs)


def ring_pairs(length, step):
    ring = [0] + list(range(1, length, 2)) + list(range(2, length, 2))[::-1]
    return [
        (ring[k] * PLANE + lo, ring[(k + step) % length] * PLANE + lo)
        for k in range(length)
        for lo in range(PLANE)
    ]


def local(tokens, expert_ids, gate_weights, out_grad, w_in, w_out):
    count = lax.axis_size(AXIS)
    length = count // PLANE
    tok_count, _ = tokens.shape
    cap = 6 * tok_count // count
    me = jnp.stack([lax.axis_index(AXIS)]).astype(jnp.int32)
    order = Order()
    onward = ring_pairs(length, 1)
    core, side = ([(i, i ^ p) for i in range(count)] for p in (1, 2))
    routes, slopes = {}, {}

    def send(value, pairs, *after):
        return permute(lax.optimization_barrier((value, order.last, after))[0], pairs)

    class Tensor:
        def __init__(self, block, first):
            self.first, self.block = first, {0: block}
            self.other, self.mine, self.away = {}, {}, {}
            self.outs, self.rows, self.kept, self.crossed = {}, {}, {}, {}
            self.moving = None

        def step(self, t):
            if t < length:
                self.block[t] = send(self.block[t - 1], onward)

        def swap(self, t):
            self.other[t] = send(self.block[t], core)

        def pick(self, t):
            found = None if self.first else routes[t]
            rows, new = select(order, me, [self.block[t], self.other[t]], cap, found)
            if self.first:
                routes[t] = new
            self.mine[t], self.away[t] = rows[0], send(rows[1], side)

        def serve(self, t):
            slope = None if self.first else slopes[t]
            self.outs[t], kept = expert_pass(order, self.mine[t], self.away[t], w_in, w_out, slope)
            self.kept[t] = kept[:2]
            if self.first:
                slopes[t] = kept[2]

        def back(self, t):
            self.rows[t] = [self.outs[t][0], send(self.outs[t][1], side)]

        def cross(self, t):
            self.crossed[t] = send(combine(order, self.rows[t], routes[t], 1, self.first), core)

        def fold(self, t):
            extras = [self.crossed[t]] + ([] if self.moving is None else [self.moving])
            sums = combine(order, self.rows[t], routes[t], 0, self.first, extras)
            self.moving = send(sums, onward) if t else sums

    x = Tensor(stack_block(order, tokens, expert_ids, gate_weights), True)
    grad = Tensor(out_grad, False)
    both = (x, grad)
    for tensor in both:
        tensor.step(1)
        tensor.swap(0)
    for tensor in both:
        tensor.pick(0)
    for t in range(1, length):
        for tensor in both:
            tensor.step(t + 1)
            tensor.swap(t)
            tensor.serve(t - 1)
            if t > 1:
                tensor.back(t - 1)
            if t > 2:
                tensor.cross(t - 2)
            tensor.pick(t)
            if t > 2:
                tensor.fold(t - 2)
    top = length - 1
    x.cross(top - 1)
    x.serve(top)
    x.back(top)
    x.fold(top - 1)
    grad.cross(top - 1)
    grad.serve(top)
    grad.back(top)
    grad.fold(top - 1)
    x.back(0)
    grad.back(0)
    every = range(length)
    w_out_grad = weight_grad(
        order, [x.kept[t][1] for t in every], [grad.kept[t][0] for t in every], 512, True, "weights_out"
    )
    x.cross(top)
    grad.cross(top)
    x.fold(top)
    grad.fold(top)
    w_in_grad = weight_grad(
        order, [x.kept[t][0] for t in every], [grad.kept[t][1] for t in every], 512, False, "weights_in"
    )
    for tensor in both:
        tensor.cross(0)
    for tensor in both:
        tensor.fold(0)
    return x.moving, grad.moving, w_in_grad, w_out_grad


def solution(mesh):
    rows, wide = P(("groups", AXIS), None), P(("groups", AXIS), None, None)
    weights = P(AXIS, None, None)
    return jax.shard_map(
        local,
        mesh=mesh,
        in_specs=(rows, rows, rows, rows, weights, weights),
        out_specs=(rows, rows, wide, wide),
        check_vma=False,
    )
```

```python
import functools

import jax
import jax.numpy as jnp
from jax import lax
from jax.experimental import pallas as pl
from jax.experimental.pallas import tpu as pltpu
from jax.sharding import PartitionSpec as P

AXIS = "expert"
PLANE = 4
PAIR = 2
INV_ROOT_TWO = 0.7071067811865476
INV_ROOT_TAU = 0.3989422804014327
PEAK = 3.45e9
BF16 = jnp.bfloat16
F32 = jnp.float32
SMEM = pl.BlockSpec(memory_space=pltpu.SMEM)
VMEM = pl.BlockSpec(memory_space=pltpu.VMEM)


def params(mib):
    return pltpu.CompilerParams(vmem_limit_bytes=mib * 1024 * 1024)


def dot(a, b, dims):
    return lax.dot_general(a, b, (dims, ((), ())), preferred_element_type=F32)


META = 16


def call(
    kernel, order, operands, specs, out_shape, out_specs, name, mib=24, grid=(1,), scratch=(), cost=0.4
):
    result = pl.pallas_call(
        kernel,
        grid=grid,
        out_shape=out_shape,
        in_specs=specs,
        out_specs=out_specs,
        scratch_shapes=list(scratch),
        compiler_params=params(mib),
        cost_estimate=pl.CostEstimate(
            flops=int(cost * PEAK), bytes_accessed=1000, transcendentals=0
        ),
        name=name,
    )(*order.behind(operands))
    order.last = result[0] if isinstance(result, (tuple, list)) else result
    return result


class Order:
    def __init__(self, last=None):
        self.last = last

    def behind(self, operands):
        if self.last is None:
            return list(operands)
        return list(lax.optimization_barrier((tuple(operands), self.last))[0])


def whole(shape):
    zeros = (0,) * len(shape)
    return pl.BlockSpec(shape, lambda *i: zeros)


def stack_kernel(tokens_ref, ids_ref, gates_ref, out_ref):
    tokens, _ = tokens_ref.shape
    out_ref[:tokens, :] = tokens_ref[...]
    eye = lax.broadcasted_iota(jnp.int32, (tokens, tokens), 0) == lax.broadcasted_iota(
        jnp.int32, (tokens, tokens), 1
    )

    def as_row(column):
        return jnp.sum(jnp.where(eye, column, 0.0), axis=0, keepdims=True)

    ids, gates = ids_ref[...].astype(F32), gates_ref[...]
    rows = [as_row(ids[:, k : k + 1]) for k in range(2)]
    for k in range(2):
        rest = as_row(gates[:, k : k + 1])
        for _ in range(3):
            part = rest.astype(BF16).astype(F32)
            rows.append(part)
            rest = rest - part
    rows += rows
    out_ref[tokens:, :] = jnp.zeros((META, out_ref.shape[1]), BF16)
    out_ref[tokens:, :tokens] = jnp.concatenate(rows, axis=0).astype(BF16)


def stack_block(order, tokens, expert_ids, gate_weights):
    count, width = tokens.shape
    return call(
        stack_kernel,
        order,
        (tokens, expert_ids, gate_weights),
        [whole(tokens.shape), whole(expert_ids.shape), whole(gate_weights.shape)],
        jax.ShapeDtypeStruct((count + META, width), BF16),
        whole((count + META, width)),
        "stack_block",
    )


def route_rows(experts, meta, cap, at, pick_ref, put_ref, row_gate_ref, token_gate_ref):
    tokens = meta.shape[1]
    upper = (
        lax.broadcasted_iota(jnp.int32, (tokens, tokens), 0)
        < lax.broadcasted_iota(jnp.int32, (tokens, tokens), 1)
    ).astype(BF16)
    eye = lax.broadcasted_iota(jnp.int32, (tokens, tokens), 0) == lax.broadcasted_iota(
        jnp.int32, (tokens, tokens), 1
    )
    down = lax.broadcasted_iota(jnp.int32, (cap, tokens), 0).astype(F32)
    along = lax.broadcasted_iota(jnp.int32, (tokens, cap), 1).astype(F32)
    lane = lax.broadcasted_iota(jnp.int32, (tokens, 128), 1)
    first, second = meta[0:1], meta[1:2]
    gate_one = meta[2:3] + meta[3:4] + meta[4:5]
    gate_two = meta[5:6] + meta[6:7] + meta[7:8]
    marks, gates = [], []
    for expert in experts:
        is_one = (first == expert).astype(F32)
        is_two = (second == expert).astype(F32)
        marks.append(is_one + is_two)
        gates.append(is_one * gate_one + is_two * gate_two)
    marks = jnp.concatenate(marks * 4, axis=0)
    rank = dot(marks.astype(BF16), upper, ((1,), (0,)))
    rank = jnp.where(marks > 0.0, rank, -1.0)
    token_gate = jnp.zeros((tokens, 128), F32)
    picks = []
    for k in range(PAIR):
        row = rank[k : k + 1]
        hit = down == row
        picks.append(hit.astype(F32).astype(BF16))
        pick_ref[k, at] = picks[-1]
        gate = jnp.sum(jnp.where(hit, gates[k], 0.0), axis=1, keepdims=True)
        row_gate_ref[k, at] = jnp.broadcast_to(gate, (cap, 128))
        column = jnp.sum(jnp.where(eye, row, 0.0), axis=1, keepdims=True)
        put_ref[k, at] = (along == column).astype(F32).astype(BF16)
        gate = jnp.sum(jnp.where(eye, gates[k], 0.0), axis=1, keepdims=True)
        token_gate = jnp.where(lane == k, gate, token_gate)
    token_gate_ref[at] = token_gate
    return picks


def select_kernel(scaled, cap, me_ref, *refs):
    blocks, refs = refs[:PAIR], refs[PAIR:]
    if scaled:
        (pick_ref, row_gate_ref), refs = refs[:2], refs[2:]
    outs, routes = refs[:PAIR], refs[PAIR:]
    me = me_ref[0]
    experts = [me.astype(F32), (me ^ 2).astype(F32)]
    for at, ref in enumerate(blocks):
        if scaled:
            block = ref[...]
            picks = [pick_ref[k, at] for k in range(PAIR)]
        else:
            tokens = ref.shape[0] - META
            block = ref[:tokens, :]
            meta = ref[tokens:, :tokens].astype(F32)
            picks = route_rows(experts, meta, cap, at, *routes)
        for k in range(PAIR):
            rows = dot(picks[k], block, ((1,), (0,)))
            if scaled:
                rows = rows * row_gate_ref[k, at][:, :1]
            outs[k][at * cap : (at + 1) * cap, :] = rows.astype(BF16)


def select(order, me, blocks, cap, routes=None):
    width = blocks[0].shape[1]
    tokens = blocks[0].shape[0] - (META if routes is None else 0)
    shapes = [jax.ShapeDtypeStruct((PAIR * cap, width), BF16)] * PAIR
    operands = [me, *blocks]
    specs = [SMEM] + [whole(b.shape) for b in blocks]
    if routes is None:
        shapes += [
            jax.ShapeDtypeStruct((PAIR, PAIR, cap, tokens), BF16),
            jax.ShapeDtypeStruct((PAIR, PAIR, tokens, cap), BF16),
            jax.ShapeDtypeStruct((PAIR, PAIR, cap, 128), F32),
            jax.ShapeDtypeStruct((PAIR, tokens, 128), F32),
        ]
    else:
        operands += [routes[0], routes[2]]
        specs += [whole(routes[0].shape), whole(routes[2].shape)]
    result = call(
        functools.partial(select_kernel, routes is not None, cap),
        order,
        operands,
        specs,
        tuple(shapes),
        tuple(whole(s.shape) for s in shapes),
        "select_rows",
    )
    return result[:PAIR], result[PAIR:]


def combine_kernel(at, gated, *refs):
    rows, (put_ref, gate_ref), more, out_ref = refs[:PAIR], refs[PAIR : PAIR + 2], refs[PAIR + 2 : -1], refs[-1]
    cap = rows[0].shape[0] // PAIR
    total = None
    for k in range(PAIR):
        part = dot(put_ref[k, at], rows[k][at * cap : (at + 1) * cap, :], ((1,), (0,)))
        if gated:
            part = part * gate_ref[at][:, k : k + 1]
        total = part if total is None else total + part
    for ref in more:
        total = total + ref[...].astype(F32)
    out_ref[...] = total.astype(BF16)


def combine(order, rows, routes, at, gated, extras=()):
    operands = [*rows, routes[1], routes[3], *extras]
    shape = (routes[3].shape[1], rows[0].shape[1])
    return call(
        functools.partial(combine_kernel, at, gated),
        order,
        operands,
        [whole(o.shape) for o in operands],
        jax.ShapeDtypeStruct(shape, BF16),
        whole(shape),
        "combine_rows",
    )


def gelu_parts(pre_act):
    normal_cdf = 0.5 * (1.0 + lax.erf(pre_act * INV_ROOT_TWO))
    normal_pdf = jnp.exp(-0.5 * pre_act * pre_act) * INV_ROOT_TAU
    return (pre_act * normal_cdf, normal_cdf + pre_act * normal_pdf)


def expert_kernel(first, steps, mine_ref, side_ref, win_ref, wout_ref, *refs):
    step = pl.program_id(0)
    if first:
        my_out, side_out, rows_ref, act_ref, slope_ref, total = refs
    else:
        slope_ref, my_out, side_out, rows_ref, pre_ref, total = refs
    size = mine_ref.shape[0]

    @pl.when(step == 0)
    def _():
        rows_ref[:size, :] = mine_ref[...]
        rows_ref[size:, :] = side_ref[...]
        total[...] = jnp.zeros_like(total)

    if first:
        act, slope = gelu_parts(dot(rows_ref[...], win_ref[0], ((1,), (0,))))
        act = act.astype(BF16)
        act_ref[...] = act
        slope_ref[...] = slope
        total[...] += dot(act, wout_ref[0], ((1,), (0,)))
    else:
        act_grad = dot(rows_ref[...], wout_ref[0], ((1,), (1,)))
        pre_grad = (act_grad * slope_ref[...]).astype(BF16)
        pre_ref[...] = pre_grad
        total[...] += dot(pre_grad, win_ref[0], ((1,), (1,)))

    @pl.when(step == steps - 1)
    def _():
        my_out[...] = total[:size, :].astype(BF16)
        side_out[...] = total[size:, :].astype(BF16)


def expert_pass(order, mine, side, w_in, w_out, slope=None, tile=512):
    first = slope is None
    width, hidden = w_in.shape[1:]
    size = mine.shape[0]
    steps = hidden // tile
    part = pl.BlockSpec((2 * size, tile), lambda f: (0, f))
    shapes = [jax.ShapeDtypeStruct((size, width), BF16)] * 2
    shapes += [jax.ShapeDtypeStruct((2 * size, width), BF16)]
    shapes += [jax.ShapeDtypeStruct((2 * size, hidden), BF16)]
    shapes += [jax.ShapeDtypeStruct((2 * size, hidden), F32)] if first else []
    result = call(
        functools.partial(expert_kernel, first, steps),
        order,
        [mine, side, w_in, w_out] + ([] if first else [slope]),
        [whole(mine.shape), whole(side.shape)]
        + [
            pl.BlockSpec((1, width, tile), lambda f: (0, 0, f)),
            pl.BlockSpec((1, tile, width), lambda f: (0, f, 0)),
        ]
        + ([] if first else [part]),
        tuple(shapes),
        tuple(whole(k.shape) for k in shapes[:3]) + (part,) * (len(shapes) - 3),
        "expert_forward" if first else "expert_backward",
        mib=32,
        grid=(steps,),
        scratch=[pltpu.VMEM((2 * size, width), F32)],
        cost=5.0,
    )
    return result[:2], result[2:]


def weight_kernel(count, *refs):
    total = None
    for a, b in zip(refs[:count], refs[count : 2 * count]):
        part = dot(a[...], b[...], ((0,), (0,)))
        total = part if total is None else total + part
    refs[-1][0] = total.astype(BF16)


def weight_grad(after, lefts, rights, tile, by_left, name):
    m, n = lefts[0].shape[1], rights[0].shape[1]

    def spec(array, tiled):
        rows, columns = array.shape
        if tiled:
            return pl.BlockSpec((rows, tile), lambda f: (0, f))
        return pl.BlockSpec((rows, columns), lambda f: (0, 0))

    return call(
        functools.partial(weight_kernel, len(lefts)),
        Order(after),
        [*lefts, *rights],
        [spec(a, by_left) for a in lefts] + [spec(b, not by_left) for b in rights],
        jax.ShapeDtypeStruct((1, m, n), BF16),
        pl.BlockSpec((1, tile, n), lambda f: (0, f, 0))
        if by_left
        else pl.BlockSpec((1, m, tile), lambda f: (0, 0, f)),
        name,
        mib=44,
        cost=10.0,
        grid=((m if by_left else n) // tile,),
    )


def permute(value, pairs):
    return lax.ppermute(value, AXIS, pairs)


def ring_pairs(length, step):
    ring = [0] + list(range(1, length, 2)) + list(range(2, length, 2))[::-1]
    return [
        (ring[k] * PLANE + lo, ring[(k + step) % length] * PLANE + lo)
        for k in range(length)
        for lo in range(PLANE)
    ]


def local(tokens, expert_ids, gate_weights, out_grad, w_in, w_out):
    count = lax.axis_size(AXIS)
    length = count // PLANE
    tok_count, _ = tokens.shape
    cap = 6 * tok_count // count
    me = jnp.stack([lax.axis_index(AXIS)]).astype(jnp.int32)
    order = Order()
    onward = ring_pairs(length, 1)
    core, side = ([(i, i ^ p) for i in range(count)] for p in (1, 2))
    routes, slopes = {}, {}

    def send(value, pairs, *after):
        return permute(lax.optimization_barrier((value, order.last, after))[0], pairs)

    class Tensor:
        def __init__(self, block, first):
            self.first, self.block = first, {0: block}
            self.other, self.mine, self.away = {}, {}, {}
            self.outs, self.rows, self.kept, self.crossed = {}, {}, {}, {}
            self.moving = None

        def step(self, t):
            if t < length:
                self.block[t] = send(self.block[t - 1], onward)

        def swap(self, t):
            self.other[t] = send(self.block[t], core)

        def pick(self, t):
            found = None if self.first else routes[t]
            rows, new = select(order, me, [self.block[t], self.other[t]], cap, found)
            if self.first:
                routes[t] = new
            self.mine[t], self.away[t] = rows[0], send(rows[1], side)

        def serve(self, t):
            slope = None if self.first else slopes[t]
            self.outs[t], kept = expert_pass(order, self.mine[t], self.away[t], w_in, w_out, slope)
            self.kept[t] = kept[:2]
            if self.first:
                slopes[t] = kept[2]

        def back(self, t):
            self.rows[t] = [self.outs[t][0], send(self.outs[t][1], side)]

        def cross(self, t):
            self.crossed[t] = send(combine(order, self.rows[t], routes[t], 1, self.first), core)

        def fold(self, t):
            extras = [self.crossed[t]] + ([] if self.moving is None else [self.moving])
            sums = combine(order, self.rows[t], routes[t], 0, self.first, extras)
            self.moving = send(sums, onward) if t else sums

    x = Tensor(stack_block(order, tokens, expert_ids, gate_weights), True)
    grad = Tensor(out_grad, False)
    both = (x, grad)
    for tensor in both:
        tensor.step(1)
        tensor.swap(0)
    for tensor in both:
        tensor.pick(0)
    for t in range(1, length):
        for tensor in both:
            tensor.step(t + 1)
            tensor.swap(t)
            tensor.serve(t - 1)
            if t > 1:
                tensor.back(t - 1)
            if t > 2:
                tensor.cross(t - 2)
            tensor.pick(t)
            if t > 2:
                tensor.fold(t - 2)
    top = length - 1
    x.cross(top - 1)
    x.serve(top)
    x.back(top)
    x.fold(top - 1)
    grad.cross(top - 1)
    grad.serve(top)
    grad.back(top)
    grad.fold(top - 1)
    x.back(0)
    grad.back(0)
    every = range(length)
    x.cross(top)
    grad.cross(top)
    x.fold(top)
    grad.fold(top)
    after = order.last
    w_out_grad = weight_grad(
        None, [x.kept[t][1] for t in every], [grad.kept[t][0] for t in every], 512, True, "weights_out"
    )
    w_in_grad = weight_grad(
        after, [x.kept[t][0] for t in every], [grad.kept[t][1] for t in every], 512, False, "weights_in"
    )
    x.cross(0)
    grad.cross(0)
    x.fold(0)
    grad.fold(0)
    return x.moving, grad.moving, w_in_grad, w_out_grad


def solution(mesh):
    rows, wide = P(("groups", AXIS), None), P(("groups", AXIS), None, None)
    weights = P(AXIS, None, None)
    return jax.shard_map(
        local,
        mesh=mesh,
        in_specs=(rows, rows, rows, rows, weights, weights),
        out_specs=(rows, rows, wide, wide),
        check_vma=False,
    )
```

```python
import functools

import jax
import jax.numpy as jnp
from jax import lax
from jax.experimental import pallas as pl
from jax.experimental.pallas import tpu as pltpu
from jax.sharding import PartitionSpec as P

AXIS = "expert"
PLANE = 4
PAIR = 2
INV_ROOT_TWO = 0.7071067811865476
INV_ROOT_TAU = 0.3989422804014327
PEAK = 5.2e9
BF16 = jnp.bfloat16
F32 = jnp.float32
SMEM = pl.BlockSpec(memory_space=pltpu.SMEM)
VMEM = pl.BlockSpec(memory_space=pltpu.VMEM)


def params(mib):
    return pltpu.CompilerParams(vmem_limit_bytes=mib * 1024 * 1024)


def dot(a, b, dims):
    return lax.dot_general(a, b, (dims, ((), ())), preferred_element_type=F32)


META = 16


def call(
    kernel, order, operands, specs, out_shape, out_specs, name, mib=24, grid=(1,), scratch=(), cost=0.4
):
    result = pl.pallas_call(
        kernel,
        grid=grid,
        out_shape=out_shape,
        in_specs=specs,
        out_specs=out_specs,
        scratch_shapes=list(scratch),
        compiler_params=params(mib),
        cost_estimate=pl.CostEstimate(
            flops=int(cost * PEAK), bytes_accessed=1000, transcendentals=0
        ),
        name=name,
    )(*order.behind(operands))
    order.last = result[0] if isinstance(result, (tuple, list)) else result
    return result


class Order:
    def __init__(self, last=None):
        self.last = last

    def behind(self, operands):
        if self.last is None:
            return list(operands)
        return list(lax.optimization_barrier((tuple(operands), self.last))[0])


def whole(shape):
    zeros = (0,) * len(shape)
    return pl.BlockSpec(shape, lambda *i: zeros)


def stack_kernel(tokens_ref, ids_ref, gates_ref, out_ref):
    tokens, _ = tokens_ref.shape
    out_ref[:tokens, :] = tokens_ref[...]
    eye = lax.broadcasted_iota(jnp.int32, (tokens, tokens), 0) == lax.broadcasted_iota(
        jnp.int32, (tokens, tokens), 1
    )

    def as_row(column):
        return jnp.sum(jnp.where(eye, column, 0.0), axis=0, keepdims=True)

    ids, gates = ids_ref[...].astype(F32), gates_ref[...]
    rows = [as_row(ids[:, k : k + 1]) for k in range(2)]
    for k in range(2):
        rest = as_row(gates[:, k : k + 1])
        for _ in range(3):
            part = rest.astype(BF16).astype(F32)
            rows.append(part)
            rest = rest - part
    rows += rows
    out_ref[tokens:, :] = jnp.zeros((META, out_ref.shape[1]), BF16)
    out_ref[tokens:, :tokens] = jnp.concatenate(rows, axis=0).astype(BF16)


def stack_block(order, tokens, expert_ids, gate_weights):
    count, width = tokens.shape
    return call(
        stack_kernel,
        order,
        (tokens, expert_ids, gate_weights),
        [whole(tokens.shape), whole(expert_ids.shape), whole(gate_weights.shape)],
        jax.ShapeDtypeStruct((count + META, width), BF16),
        whole((count + META, width)),
        "stack_block",
    )


def route_rows(experts, meta, cap, at, pick_ref, put_ref, row_gate_ref, token_gate_ref):
    tokens = meta.shape[1]
    upper = (
        lax.broadcasted_iota(jnp.int32, (tokens, tokens), 0)
        < lax.broadcasted_iota(jnp.int32, (tokens, tokens), 1)
    ).astype(BF16)
    eye = lax.broadcasted_iota(jnp.int32, (tokens, tokens), 0) == lax.broadcasted_iota(
        jnp.int32, (tokens, tokens), 1
    )
    down = lax.broadcasted_iota(jnp.int32, (cap, tokens), 0).astype(F32)
    along = lax.broadcasted_iota(jnp.int32, (tokens, cap), 1).astype(F32)
    lane = lax.broadcasted_iota(jnp.int32, (tokens, 128), 1)
    first, second = meta[0:1], meta[1:2]
    gate_one = meta[2:3] + meta[3:4] + meta[4:5]
    gate_two = meta[5:6] + meta[6:7] + meta[7:8]
    marks, gates = [], []
    for expert in experts:
        is_one = (first == expert).astype(F32)
        is_two = (second == expert).astype(F32)
        marks.append(is_one + is_two)
        gates.append(is_one * gate_one + is_two * gate_two)
    marks = jnp.concatenate(marks * 4, axis=0)
    rank = dot(marks.astype(BF16), upper, ((1,), (0,)))
    rank = jnp.where(marks > 0.0, rank, -1.0)
    token_gate = jnp.zeros((tokens, 128), F32)
    picks = []
    for k in range(PAIR):
        row = rank[k : k + 1]
        hit = down == row
        picks.append(hit.astype(F32).astype(BF16))
        pick_ref[k, at] = picks[-1]
        gate = jnp.sum(jnp.where(hit, gates[k], 0.0), axis=1, keepdims=True)
        row_gate_ref[k, at] = jnp.broadcast_to(gate, (cap, 128))
        column = jnp.sum(jnp.where(eye, row, 0.0), axis=1, keepdims=True)
        put_ref[k, at] = (along == column).astype(F32).astype(BF16)
        gate = jnp.sum(jnp.where(eye, gates[k], 0.0), axis=1, keepdims=True)
        token_gate = jnp.where(lane == k, gate, token_gate)
    token_gate_ref[at] = token_gate
    return picks


def select_kernel(scaled, cap, me_ref, *refs):
    blocks, refs = refs[:PAIR], refs[PAIR:]
    if scaled:
        (pick_ref, row_gate_ref), refs = refs[:2], refs[2:]
    outs, routes = refs[:PAIR], refs[PAIR:]
    me = me_ref[0]
    experts = [me.astype(F32), (me ^ 2).astype(F32)]
    for at, ref in enumerate(blocks):
        if scaled:
            block = ref[...]
            picks = [pick_ref[k, at] for k in range(PAIR)]
        else:
            tokens = ref.shape[0] - META
            block = ref[:tokens, :]
            meta = ref[tokens:, :tokens].astype(F32)
            picks = route_rows(experts, meta, cap, at, *routes)
        for k in range(PAIR):
            rows = dot(picks[k], block, ((1,), (0,)))
            if scaled:
                rows = rows * row_gate_ref[k, at][:, :1]
            outs[k][at * cap : (at + 1) * cap, :] = rows.astype(BF16)


def select(order, me, blocks, cap, routes=None):
    width = blocks[0].shape[1]
    tokens = blocks[0].shape[0] - (META if routes is None else 0)
    shapes = [jax.ShapeDtypeStruct((PAIR * cap, width), BF16)] * PAIR
    operands = [me, *blocks]
    specs = [SMEM] + [whole(b.shape) for b in blocks]
    if routes is None:
        shapes += [
            jax.ShapeDtypeStruct((PAIR, PAIR, cap, tokens), BF16),
            jax.ShapeDtypeStruct((PAIR, PAIR, tokens, cap), BF16),
            jax.ShapeDtypeStruct((PAIR, PAIR, cap, 128), F32),
            jax.ShapeDtypeStruct((PAIR, tokens, 128), F32),
        ]
    else:
        operands += [routes[0], routes[2]]
        specs += [whole(routes[0].shape), whole(routes[2].shape)]
    result = call(
        functools.partial(select_kernel, routes is not None, cap),
        order,
        operands,
        specs,
        tuple(shapes),
        tuple(whole(s.shape) for s in shapes),
        "select_rows",
    )
    return result[:PAIR], result[PAIR:]


def combine_kernel(at, gated, *refs):
    rows, (put_ref, gate_ref), more, out_ref = refs[:PAIR], refs[PAIR : PAIR + 2], refs[PAIR + 2 : -1], refs[-1]
    cap = rows[0].shape[0] // PAIR
    total = None
    for k in range(PAIR):
        part = dot(put_ref[k, at], rows[k][at * cap : (at + 1) * cap, :], ((1,), (0,)))
        if gated:
            part = part * gate_ref[at][:, k : k + 1]
        total = part if total is None else total + part
    for ref in more:
        total = total + ref[...].astype(F32)
    out_ref[...] = total.astype(BF16)


def combine(order, rows, routes, at, gated, extras=()):
    operands = [*rows, routes[1], routes[3], *extras]
    shape = (routes[3].shape[1], rows[0].shape[1])
    return call(
        functools.partial(combine_kernel, at, gated),
        order,
        operands,
        [whole(o.shape) for o in operands],
        jax.ShapeDtypeStruct(shape, BF16),
        whole(shape),
        "combine_rows",
    )


def gelu_parts(pre_act):
    normal_cdf = 0.5 * (1.0 + lax.erf(pre_act * INV_ROOT_TWO))
    normal_pdf = jnp.exp(-0.5 * pre_act * pre_act) * INV_ROOT_TAU
    return (pre_act * normal_cdf, normal_cdf + pre_act * normal_pdf)


def expert_kernel(first, steps, mine_ref, side_ref, win_ref, wout_ref, *refs):
    step = pl.program_id(0)
    if first:
        my_out, side_out, rows_ref, act_ref, slope_ref, total = refs
    else:
        slope_ref, my_out, side_out, rows_ref, pre_ref, total = refs
    size = mine_ref.shape[0]

    @pl.when(step == 0)
    def _():
        rows_ref[:size, :] = mine_ref[...]
        rows_ref[size:, :] = side_ref[...]
        total[...] = jnp.zeros_like(total)

    if first:
        act, slope = gelu_parts(dot(rows_ref[...], win_ref[0], ((1,), (0,))))
        act = act.astype(BF16)
        act_ref[...] = act
        slope_ref[...] = slope
        total[...] += dot(act, wout_ref[0], ((1,), (0,)))
    else:
        act_grad = dot(rows_ref[...], wout_ref[0], ((1,), (1,)))
        pre_grad = (act_grad * slope_ref[...]).astype(BF16)
        pre_ref[...] = pre_grad
        total[...] += dot(pre_grad, win_ref[0], ((1,), (1,)))

    @pl.when(step == steps - 1)
    def _():
        my_out[...] = total[:size, :].astype(BF16)
        side_out[...] = total[size:, :].astype(BF16)


def expert_pass(order, mine, side, w_in, w_out, slope=None, tile=512):
    first = slope is None
    width, hidden = w_in.shape[1:]
    size = mine.shape[0]
    steps = hidden // tile
    part = pl.BlockSpec((2 * size, tile), lambda f: (0, f))
    shapes = [jax.ShapeDtypeStruct((size, width), BF16)] * 2
    shapes += [jax.ShapeDtypeStruct((2 * size, width), BF16)]
    shapes += [jax.ShapeDtypeStruct((2 * size, hidden), BF16)]
    shapes += [jax.ShapeDtypeStruct((2 * size, hidden), F32)] if first else []
    result = call(
        functools.partial(expert_kernel, first, steps),
        order,
        [mine, side, w_in, w_out] + ([] if first else [slope]),
        [whole(mine.shape), whole(side.shape)]
        + [
            pl.BlockSpec((1, width, tile), lambda f: (0, 0, f)),
            pl.BlockSpec((1, tile, width), lambda f: (0, f, 0)),
        ]
        + ([] if first else [part]),
        tuple(shapes),
        tuple(whole(k.shape) for k in shapes[:3]) + (part,) * (len(shapes) - 3),
        "expert_forward" if first else "expert_backward",
        mib=32,
        grid=(steps,),
        scratch=[pltpu.VMEM((2 * size, width), F32)],
        cost=5.0,
    )
    return result[:2], result[2:]


def weight_kernel(count, *refs):
    total = None
    for a, b in zip(refs[:count], refs[count : 2 * count]):
        part = dot(a[...], b[...], ((0,), (0,)))
        total = part if total is None else total + part
    refs[-1][0] = total.astype(BF16)


def weight_grad(after, lefts, rights, tile, by_left, name):
    m, n = lefts[0].shape[1], rights[0].shape[1]

    def spec(array, tiled):
        rows, columns = array.shape
        if tiled:
            return pl.BlockSpec((rows, tile), lambda f: (0, f))
        return pl.BlockSpec((rows, columns), lambda f: (0, 0))

    return call(
        functools.partial(weight_kernel, len(lefts)),
        Order(after),
        [*lefts, *rights],
        [spec(a, by_left) for a in lefts] + [spec(b, not by_left) for b in rights],
        jax.ShapeDtypeStruct((1, m, n), BF16),
        pl.BlockSpec((1, tile, n), lambda f: (0, f, 0))
        if by_left
        else pl.BlockSpec((1, m, tile), lambda f: (0, 0, f)),
        name,
        mib=44,
        cost=10.0,
        grid=((m if by_left else n) // tile,),
    )


def permute(value, pairs):
    return lax.ppermute(value, AXIS, pairs)


def ring_pairs(length, step):
    ring = [0] + list(range(1, length, 2)) + list(range(2, length, 2))[::-1]
    return [
        (ring[k] * PLANE + lo, ring[(k + step) % length] * PLANE + lo)
        for k in range(length)
        for lo in range(PLANE)
    ]


def local(tokens, expert_ids, gate_weights, out_grad, w_in, w_out):
    count = lax.axis_size(AXIS)
    length = count // PLANE
    tok_count, _ = tokens.shape
    cap = 6 * tok_count // count
    me = jnp.stack([lax.axis_index(AXIS)]).astype(jnp.int32)
    order = Order()
    onward = ring_pairs(length, 1)
    core, side = ([(i, i ^ p) for i in range(count)] for p in (1, 2))
    routes, slopes = {}, {}

    def send(value, pairs, *after):
        return permute(lax.optimization_barrier((value, order.last, after))[0], pairs)

    class Tensor:
        def __init__(self, block, first):
            self.first, self.block = first, {0: block}
            self.other, self.mine, self.away = {}, {}, {}
            self.outs, self.rows, self.kept, self.crossed = {}, {}, {}, {}
            self.moving = None

        def step(self, t):
            if t < length:
                self.block[t] = send(self.block[t - 1], onward)

        def swap(self, t):
            self.other[t] = send(self.block[t], core)

        def pick(self, t):
            found = None if self.first else routes[t]
            rows, new = select(order, me, [self.block[t], self.other[t]], cap, found)
            if self.first:
                routes[t] = new
            self.mine[t], self.away[t] = rows[0], send(rows[1], side)

        def serve(self, t):
            slope = None if self.first else slopes[t]
            self.outs[t], kept = expert_pass(order, self.mine[t], self.away[t], w_in, w_out, slope)
            self.kept[t] = kept[:2]
            if self.first:
                slopes[t] = kept[2]

        def back(self, t):
            self.rows[t] = [self.outs[t][0], send(self.outs[t][1], side)]

        def cross(self, t):
            self.crossed[t] = send(combine(order, self.rows[t], routes[t], 1, self.first), core)

        def fold(self, t):
            extras = [self.crossed[t]] + ([] if self.moving is None else [self.moving])
            sums = combine(order, self.rows[t], routes[t], 0, self.first, extras)
            self.moving = send(sums, onward) if t else sums

    x = Tensor(stack_block(order, tokens, expert_ids, gate_weights), True)
    grad = Tensor(out_grad, False)
    both = (x, grad)
    for tensor in both:
        tensor.step(1)
        tensor.swap(0)
    for tensor in both:
        tensor.pick(0)
    for t in range(1, length):
        for tensor in both:
            tensor.step(t + 1)
            tensor.swap(t)
            tensor.serve(t - 1)
            if t > 2:
                tensor.cross(t - 2)
            tensor.pick(t)
            if t > 1:
                tensor.back(t - 1)
            if t > 2:
                tensor.fold(t - 2)
    top = length - 1
    x.cross(top - 1)
    x.serve(top)
    x.back(top)
    x.fold(top - 1)
    grad.cross(top - 1)
    grad.serve(top)
    grad.back(top)
    grad.fold(top - 1)
    x.back(0)
    grad.back(0)
    every = range(length)
    x.cross(top)
    grad.cross(top)
    x.fold(top)
    grad.fold(top)
    after = order.last
    w_out_grad = weight_grad(
        None, [x.kept[t][1] for t in every], [grad.kept[t][0] for t in every], 512, True, "weights_out"
    )
    w_in_grad = weight_grad(
        after, [x.kept[t][0] for t in every], [grad.kept[t][1] for t in every], 512, False, "weights_in"
    )
    x.cross(0)
    grad.cross(0)
    x.fold(0)
    grad.fold(0)
    return x.moving, grad.moving, w_in_grad, w_out_grad


def solution(mesh):
    rows, wide = P(("groups", AXIS), None), P(("groups", AXIS), None, None)
    weights = P(AXIS, None, None)
    return jax.shard_map(
        local,
        mesh=mesh,
        in_specs=(rows, rows, rows, rows, weights, weights),
        out_specs=(rows, rows, wide, wide),
        check_vma=False,
    )
```
